32 devices in a mesh: rows: 8 (over z, core), delay: 4 (over y, x).
Axes of the slice: x: 2, y: 2, z: 4, core: 2. Of those that a mesh axis runs over, the one named last changes fastest.
Arguments:
- retarded_tiles: bfloat16 [4, 512, 4, 128, 128], P('delay', 'rows'), may hold values from -0.125 to 0.125
- wanted_blocks: int32 [4, 8, 8, 16], P('delay', 'rows'), may hold values from 0 to 63, as said below
- tile_slots: int32 [4, 512, 4], P('delay', 'rows'), may hold values from 0 to 127, as said below
- diag_inverse: bfloat16 [512, 128, 128], P('rows')
- excitation: float32 [4, 512, 4, 128], P(None, 'rows'), may hold values from -6 to 6
- history_init: bfloat16 [4, 512, 4, 128], P('delay', 'rows'), may hold values from -6 to 6
Outputs:
- currents: float32 [4, 512, 4, 128], P(None, 'rows')
The draws below stay inside these ranges and needn't reach their ends.
Inputs may be any that keep to these rules, and one draw needn't show every extreme that they name: `wanted_blocks`: for each bin, reader and owner, 16 distinct local block numbers of the owner. `tile_slots`: in each bin, every one of a reader's 8 * 16 taken blocks is the column block of at least one tile of the reader's row blocks.
All inputs are finite; a program needn't handle non-finite values.
Results may differ from the reference program's by a relative error of at most 0.0035.
Values may be sent and summed in bfloat16 or wider, within the bound.
A program may use at most 64 MiB of HBM per device.

```python
import math
import jax
import jax.numpy as jnp
from jax import lax

B = 128
NB_DEV = 64
L = 4
EXC = 4
STEPS = 4
BINS = 4
N_BLK = 512
CAP = 16
N_ROWS = 8


def draw_wanted_blocks(key, part):
    scores = jax.random.randint(key, (BINS, N_ROWS, N_ROWS, NB_DEV), 0, 4096) * NB_DEV + jnp.arange(NB_DEV, dtype=jnp.int32)
    ranking = jnp.argsort(scores, axis=-1)
    return ranking[..., :CAP].astype(jnp.int32)


def draw_tile_slots(key, part):
    key_order = jax.random.fold_in(key, 11)
    key_fill = jax.random.fold_in(key, 12)
    spot_count = NB_DEV * L
    received = N_ROWS * CAP
    scores = jax.random.randint(key_order, (BINS, N_ROWS, spot_count), 0, 4096) * spot_count + jnp.arange(spot_count, dtype=jnp.int32)
    ranking = jnp.argsort(scores, axis=-1).astype(jnp.int32)
    filler = jax.random.randint(key_fill, (BINS, N_ROWS, spot_count), 0, received)
    values = jnp.where(ranking < received, ranking, filler)
    return values.reshape(BINS, N_BLK, L).astype(jnp.int32)


def draw_diag_inverse(key, part):
    noise = jax.random.normal(key, (N_BLK, B, B), jnp.float32)
    identity = jnp.eye(B, dtype=jnp.float32)
    return (identity + 0.3 * noise / math.sqrt(B)).astype(jnp.bfloat16)


def block_levels(stream_key, shape, cuts, low, largest):
    def one(axis_at, parts):
        steps = jax.random.uniform(jax.random.fold_in(jax.random.fold_in(stream_key, 6), axis_at), (parts,), jnp.float32, low / len(cuts), largest / len(cuts))
        return jnp.repeat(jnp.exp(steps), shape[axis_at] // parts).reshape((-1,) + (1,) * (len(shape) - axis_at - 1))

    loudness = one(*cuts[0])
    for cut in cuts[1:]:
        loudness = loudness * one(*cut)
    return loudness


def bell_draw(stream_key, dims, scale, most, split=(), kind=jnp.bfloat16):
    result = jax.random.normal(stream_key, dims, jnp.float32) * scale
    if len(split) > 0:
        result = block_levels(stream_key, dims, split, -0.22, 0.18) * result
    return jnp.clip(result, min=-most, max=most).astype(kind)


def setup_inputs(seed: int = 0) -> dict:
    seeds = jax.random.split(jax.random.key(seed), 7)
    retarded_tiles = bell_draw(seeds[0], (BINS, N_BLK, L, B, B), (B * L * BINS) ** -0.5, 0.125, ((0, 4), (1, 8)))
    wanted_blocks = draw_wanted_blocks(jax.random.fold_in(seeds[6], 71), 0)
    tile_slots = draw_tile_slots(jax.random.fold_in(seeds[6], 71), 0)
    diag_inverse = draw_diag_inverse(jax.random.fold_in(seeds[6], 71), 0)
    excitation = bell_draw(seeds[4], (STEPS, N_BLK, EXC, B), 1.0, 6.0, ((1, 8),), jnp.float32)
    history_init = bell_draw(seeds[5], (BINS, N_BLK, EXC, B), 1.0, 6.0, ((0, 4), (1, 8)))
    return {"retarded_tiles": retarded_tiles, "wanted_blocks": wanted_blocks, "tile_slots": tile_slots, "diag_inverse": diag_inverse, "excitation": excitation, "history_init": history_init}


def bin_term(hist_bin, tile_bin, column_bin):
    blocks = hist_bin[column_bin.astype(jnp.int32)].astype(jnp.float32)
    return jnp.einsum('nleb,nlbc->nec', blocks, tile_bin.astype(jnp.float32))


def reference(retarded_tiles, wanted_blocks, tile_slots, diag_inverse, excitation, history_init):
    owners = tile_slots // CAP
    within = tile_slots % CAP
    readers = (jnp.arange(N_BLK, dtype=jnp.int32) // NB_DEV)[None, :, None]
    bin_index = jnp.arange(BINS, dtype=jnp.int32)[:, None, None]
    columns = (owners * NB_DEV + wanted_blocks[bin_index, readers, owners, within]).astype(jnp.int32)
    history = history_init
    results = []
    for moment in range(STEPS):
        def add_bin(total, item):
            hist_bin, tile_bin, column_bin = item
            return total + bin_term(hist_bin, tile_bin, column_bin), None

        retarded, _ = lax.scan(add_bin, jnp.zeros((N_BLK, EXC, B), jnp.float32), (history, retarded_tiles, columns))
        driven = (excitation[moment] - retarded).astype(jnp.bfloat16)
        solved = jnp.einsum('neb,nbc->nec', driven.astype(jnp.float32), diag_inverse.astype(jnp.float32))
        results.append(solved)
        history = jnp.concatenate([solved.astype(jnp.bfloat16)[None], history[:-1]], axis=0)
    return jnp.stack(results)
```

```python
import functools

import jax
import jax.numpy as jnp
from jax import lax
from jax.experimental import pallas as pl
from jax.experimental.pallas import tpu as pltpu
from jax.sharding import PartitionSpec as P

MESH = pl.DeviceIdType.MESH
F32 = jnp.float32
BF16 = jnp.bfloat16


def row_of(shape):
    return lax.broadcasted_iota(jnp.int32, shape, 0)


def lane_of(shape):
    return lax.broadcasted_iota(jnp.int32, shape, 1)


def dot(a, b):
    return jnp.dot(a, b, preferred_element_type=F32)


def kernel(
    sizes,
    history, wanted, slots, tiles_hbm, diag_hbm, excitation_hbm,
    out,
    tiles, diag, excitation, picks, spots, ask_out, ask_in, source, sent, got, lhs,
    part_out, part_in, driven,
    load_sem, ask_send, ask_recv, shift_send, shift_recv, swap_send, swap_recv,
    part_send, part_recv, driven_send, driven_recv,
):
    readers, bins, steps, n, listed, exc, cap, width = sizes
    me = lax.axis_index("rows")
    bin_at = lax.axis_index("delay")
    rows = n * exc
    chunk = cap * exc
    group = 16 // exc
    groups = rows // 16

    loads = [
        pltpu.make_async_copy(excitation_hbm, excitation, load_sem.at[0]),
        pltpu.make_async_copy(tiles_hbm, tiles, load_sem.at[1]),
        pltpu.make_async_copy(diag_hbm, diag, load_sem.at[2]),
    ]
    for load in loads:
        load.start()

    barrier = pltpu.get_barrier_semaphore()
    for d in range(1, readers):
        pl.semaphore_signal(barrier, inc=1, device_id={"rows": lax.rem(me + d, readers)}, device_id_type=MESH)
    for d in range(1, bins):
        pl.semaphore_signal(barrier, inc=1, device_id={"delay": lax.rem(bin_at + d, bins)}, device_id_type=MESH)

    total = readers * cap
    shape = (total, readers)
    spread = jnp.where(lax.div(row_of(shape), cap) == lane_of(shape), 1.0, 0.0).astype(F32)
    every = dot(spread, wanted[...].astype(F32))
    shape = (total, cap)
    own = jnp.where(lax.rem(row_of(shape), cap) == lane_of(shape), every, 0.0)
    ask_out[...] = jnp.broadcast_to(jnp.sum(own, axis=1, keepdims=True), (total, width))

    pl.semaphore_wait(barrier, readers - 1 + bins - 1)

    def ask(d):
        peer = lax.rem(me + d, readers)
        return pltpu.make_async_remote_copy(
            src_ref=ask_out.at[pl.ds(pl.multiple_of(peer * cap, cap), cap)],
            dst_ref=ask_in.at[pl.ds(pl.multiple_of(me * cap, cap), cap)],
            send_sem=ask_send.at[d], recv_sem=ask_recv.at[d],
            device_id={"rows": peer}, device_id_type=MESH,
        )

    def asked(d):
        peer = lax.rem(me + readers - d, readers)
        there = ask_in.at[pl.ds(pl.multiple_of(peer * cap, cap), cap)]
        return pltpu.make_async_remote_copy(
            src_ref=there, dst_ref=there,
            send_sem=ask_send.at[d], recv_sem=ask_recv.at[d],
            device_id={"rows": peer}, device_id_type=MESH,
        )

    for d in range(1, readers):
        ask(d).start()

    def shift(s):
        return pltpu.make_async_remote_copy(
            src_ref=history, dst_ref=source.at[s],
            send_sem=shift_send.at[s], recv_sem=shift_recv.at[s],
            device_id={"delay": lax.rem(bin_at + s, bins)}, device_id_type=MESH,
        )

    for s in range(1, min(steps, bins)):
        @pl.when(bin_at + s < bins)
        def _():
            shift(s).start()

    mine = pl.ds(pl.multiple_of(me * cap, cap), cap)
    ask_in[mine] = ask_out[mine]
    source[0] = history[...]

    here = lax.div(row_of((rows, n)), exc) == lane_of((rows, n))
    listing = slots[...].astype(F32)
    shape = (rows, total * exc)
    lanes = lane_of(shape).astype(F32)
    which = lax.rem(row_of((rows, 1)), exc).astype(F32)
    for l in range(listed):
        slot = jnp.sum(jnp.where(here, listing[l : l + 1], 0.0), axis=1, keepdims=True)
        target = slot * exc + which
        spots[l] = jnp.where(lanes == target, 1.0, 0.0).astype(BF16)

    for d in range(1, readers):
        asked(d).wait_recv()
    shape = (total * exc, total)
    spread = jnp.where(lax.div(row_of(shape), exc) == lane_of(shape), 1.0, 0.0).astype(F32)
    target = dot(spread, ask_in[...])
    shape = (total * exc, width)
    target = target * exc + lax.rem(row_of(shape), exc).astype(F32)
    for h in range(rows // width):
        lanes = (lane_of(shape) + h * width).astype(F32)
        picks[:, h * width : (h + 1) * width] = jnp.where(lanes == target, 1.0, 0.0).astype(BF16)

    def chosen(products):
        place = lax.div(row_of((16, width)), exc)
        kept = products[:, :width]
        for i in range(1, group):
            kept = jnp.where(place == i, products[:, i * width : (i + 1) * width], kept)
        return kept

    def swap(t, d):
        peer = lax.rem(me + d, readers)
        return pltpu.make_async_remote_copy(
            src_ref=sent.at[t, pl.ds(pl.multiple_of(peer * chunk, chunk), chunk)],
            dst_ref=got.at[t, pl.ds(pl.multiple_of(me * chunk, chunk), chunk)],
            send_sem=swap_send.at[t, d], recv_sem=swap_recv.at[t, d],
            device_id={"rows": peer}, device_id_type=MESH,
        )

    def swapped(t, d):
        peer = lax.rem(me + readers - d, readers)
        there = got.at[t, pl.ds(pl.multiple_of(peer * chunk, chunk), chunk)]
        return pltpu.make_async_remote_copy(
            src_ref=there, dst_ref=there,
            send_sem=swap_send.at[t, d], recv_sem=swap_recv.at[t, d],
            device_id={"rows": peer}, device_id_type=MESH,
        )

    def part(t, k):
        return pltpu.make_async_remote_copy(
            src_ref=part_out.at[t], dst_ref=part_in.at[t, k],
            send_sem=part_send.at[t], recv_sem=part_recv.at[t, k],
            device_id={"delay": 0}, device_id_type=MESH,
        )

    def tell(t, d):
        return pltpu.make_async_remote_copy(
            src_ref=driven.at[t], dst_ref=driven.at[t],
            send_sem=driven_send.at[t, d], recv_sem=driven_recv.at[t],
            device_id={"delay": d}, device_id_type=MESH,
        )

    def solve(u):
        later = u + 1 + bin_at

        def some(q, c):
            for i in range(4):
                g = q * 4 + i
                at = pl.ds(pl.multiple_of(g * 16, 16), 16)
                right = jnp.concatenate([diag[g * group + j] for j in range(group)], axis=1)
                value = chosen(dot(driven[u, at], right))
                out[u, at] = value

                @pl.when(later < steps)
                def _():
                    source[jnp.minimum(later, steps - 1), at] = value.astype(BF16)
            return c

        lax.fori_loop(0, groups // 4, some, 0)

    def step(t, carry):
        @pl.when((t > 0) & (bin_at >= t))
        def _():
            pltpu.make_async_remote_copy(
                src_ref=history, dst_ref=source.at[t],
                send_sem=shift_send.at[t], recv_sem=shift_recv.at[t],
                device_id={"delay": lax.rem(bin_at + 1, bins)}, device_id_type=MESH,
            ).wait_recv()

        @pl.when((bin_at > 0) & (bin_at < t))
        def _():
            u = t - 1 - bin_at
            tell(u, 0).wait_recv()

            @pl.when(u == 0)
            def _():
                loads[2].wait()

            solve(u)

        sent[t] = dot(picks[...], source[t]).astype(BF16)
        for d in range(1, readers):
            swap(t, d).start()
        mine = pl.ds(pl.multiple_of(me * chunk, chunk), chunk)
        got[t, mine] = sent[t, mine]
        for d in range(1, readers):
            swapped(t, d).wait_recv()
        arrived = got[t]
        for l in range(listed):
            lhs[:, l * width : (l + 1) * width] = dot(spots[l], arrived).astype(BF16)

        @pl.when(t == 0)
        def _():
            loads[0].wait()
            loads[1].wait()

        def some(q, c):
            for i in range(4):
                g = q * 4 + i
                at = pl.ds(pl.multiple_of(g * 16, 16), 16)
                right = jnp.concatenate([tiles[g * group + j] for j in range(group)], axis=1)
                part_out[t, at] = chosen(dot(lhs[at], right))
            return c

        lax.fori_loop(0, groups // 4, some, 0)

        @pl.when(bin_at > 0)
        def _():
            part(t, bin_at).start()

        @pl.when(bin_at == 0)
        def _():
            value = part_out[t]
            for k in range(1, bins):
                part(t, k).wait_recv()
                value = value + part_in[t, k]
            driven[t] = (excitation[t] - value).astype(BF16)
            for d in range(1, bins):
                tell(t, d).start()

            @pl.when(t == 0)
            def _():
                loads[2].wait()

            solve(t)

        return carry

    lax.fori_loop(0, steps, step, 0)

    @pl.when(bin_at > 0)
    def _():
        def last(u, c):
            @pl.when(u >= steps - 1 - bin_at)
            def _():
                tell(u, 0).wait_recv()

                @pl.when(u == 0)
                def _():
                    loads[2].wait()

                solve(u)
            return c

        lax.fori_loop(0, steps, last, 0)

    for d in range(1, readers):
        ask(d).wait_send()
    for s in range(1, min(steps, bins)):
        @pl.when(bin_at + s < bins)
        def _():
            shift(s).wait_send()

    def drain(t, c):
        for d in range(1, readers):
            swap(t, d).wait_send()

        @pl.when(bin_at > 0)
        def _():
            part(t, bin_at).wait_send()

        @pl.when(bin_at == 0)
        def _():
            for d in range(1, bins):
                tell(t, d).wait_send()
        return c

    lax.fori_loop(0, steps, drain, 0)


def body(retarded_tiles, wanted_blocks, tile_slots, diag_inverse, excitation, history_init):
    readers, bins = lax.axis_size("rows"), lax.axis_size("delay")
    _, n, listed, width, _ = retarded_tiles.shape
    steps, _, exc, _ = excitation.shape
    cap = wanted_blocks.shape[-1]
    rows, taken = n * exc, readers * cap * exc
    sizes = (readers, bins, steps, n, listed, exc, cap, width)
    vmem = pl.BlockSpec(memory_space=pltpu.VMEM)
    anywhere = pl.BlockSpec(memory_space=pl.ANY)
    dma = pltpu.SemaphoreType.DMA
    solved = pl.pallas_call(
        functools.partial(kernel, sizes),
        out_shape=jax.ShapeDtypeStruct((steps, rows, width), F32),
        in_specs=[vmem, vmem, vmem, anywhere, anywhere, anywhere],
        out_specs=vmem,
        scratch_shapes=[
            pltpu.VMEM((n, listed * width, width), BF16),
            pltpu.VMEM((n, width, width), BF16),
            pltpu.VMEM((steps, rows, width), F32),
            pltpu.VMEM((taken, rows), BF16),
            pltpu.VMEM((listed, rows, taken), BF16),
            pltpu.VMEM((readers * cap, width), F32),
            pltpu.VMEM((readers * cap, width), F32),
            pltpu.VMEM((steps, rows, width), BF16),
            pltpu.VMEM((steps, taken, width), BF16),
            pltpu.VMEM((steps, taken, width), BF16),
            pltpu.VMEM((rows, listed * width), BF16),
            pltpu.VMEM((steps, rows, width), F32),
            pltpu.VMEM((steps, bins, rows, width), F32),
            pltpu.VMEM((steps, rows, width), BF16),
            dma((3,)),
            dma((readers,)),
            dma((readers,)),
            dma((steps,)),
            dma((steps,)),
            dma((steps, readers)),
            dma((steps, readers)),
            dma((steps,)),
            dma((steps, bins)),
            dma((steps, bins)),
            dma((steps,)),
        ],
        compiler_params=pltpu.CompilerParams(
            collective_id=0, has_side_effects=True, vmem_limit_bytes=57 << 20
        ),
        cost_estimate=pl.CostEstimate(
            flops=2 * steps * rows * width * width * (listed + 1), transcendentals=0,
            bytes_accessed=2 * n * width * width * (listed + 1),
        ),
    )(
        history_init.reshape(rows, width),
        wanted_blocks.reshape(readers, cap),
        tile_slots.reshape(n, listed).T,
        retarded_tiles.reshape(n, listed * width, width),
        diag_inverse,
        excitation.reshape(steps, rows, width),
    )
    return solved.reshape(steps, n, exc, width)


def solution(mesh):
    return jax.shard_map(
        body,
        mesh=mesh,
        in_specs=(
            P("delay", "rows", None, None, None),
            P("delay", "rows", None, None),
            P("delay", "rows", None),
            P("rows", None, None),
            P(None, "rows", None, None),
            P("delay", "rows", None, None),
        ),
        out_specs=P(None, "rows", None, None),
        check_vma=False,
    )
```

```python
import functools

import jax
import jax.numpy as jnp
from jax import lax
from jax.experimental import pallas as pl
from jax.experimental.pallas import tpu as pltpu
from jax.sharding import PartitionSpec as P

MESH = pl.DeviceIdType.MESH
F32 = jnp.float32
BF16 = jnp.bfloat16


def row_of(shape):
    return lax.broadcasted_iota(jnp.int32, shape, 0)


def lane_of(shape):
    return lax.broadcasted_iota(jnp.int32, shape, 1)


def dot(a, b):
    return jnp.dot(a, b, preferred_element_type=F32)


def kernel(
    sizes,
    history, wanted, slots, tiles_hbm, diag_hbm, excitation_hbm,
    out,
    tiles, diag, excitation, picks, spots, ask_out, ask_in, source, sent, got, lhs,
    part_own, part_out, part_in, driven,
    load_sem, ask_send, ask_recv, shift_send, shift_recv, swap_send, swap_recv,
    part_send, part_recv, driven_send, driven_recv,
):
    readers, bins, steps, n, listed, exc, cap, width = sizes
    me = lax.axis_index("rows")
    bin_at = lax.axis_index("delay")
    rows = n * exc
    chunk = cap * exc
    group = 16 // exc
    groups = rows // 16

    loads = [
        pltpu.make_async_copy(excitation_hbm, excitation, load_sem.at[0]),
        pltpu.make_async_copy(tiles_hbm, tiles, load_sem.at[1]),
        pltpu.make_async_copy(diag_hbm, diag, load_sem.at[2]),
    ]
    for load in loads:
        load.start()

    barrier = pltpu.get_barrier_semaphore()
    for d in range(1, readers):
        pl.semaphore_signal(barrier, inc=1, device_id={"rows": lax.rem(me + d, readers)}, device_id_type=MESH)
    for d in range(1, bins):
        pl.semaphore_signal(barrier, inc=1, device_id={"delay": lax.rem(bin_at + d, bins)}, device_id_type=MESH)

    total = readers * cap
    shape = (total, readers)
    spread = jnp.where(lax.div(row_of(shape), cap) == lane_of(shape), 1.0, 0.0).astype(F32)
    every = dot(spread, wanted[...].astype(F32))
    shape = (total, cap)
    own = jnp.where(lax.rem(row_of(shape), cap) == lane_of(shape), every, 0.0)
    ask_out[...] = jnp.broadcast_to(jnp.sum(own, axis=1, keepdims=True), (total, width))

    pl.semaphore_wait(barrier, readers - 1 + bins - 1)

    def ask(d):
        peer = lax.rem(me + d, readers)
        return pltpu.make_async_remote_copy(
            src_ref=ask_out.at[pl.ds(pl.multiple_of(peer * cap, cap), cap)],
            dst_ref=ask_in.at[pl.ds(pl.multiple_of(me * cap, cap), cap)],
            send_sem=ask_send.at[d], recv_sem=ask_recv.at[d],
            device_id={"rows": peer}, device_id_type=MESH,
        )

    def asked(d):
        peer = lax.rem(me + readers - d, readers)
        there = ask_in.at[pl.ds(pl.multiple_of(peer * cap, cap), cap)]
        return pltpu.make_async_remote_copy(
            src_ref=there, dst_ref=there,
            send_sem=ask_send.at[d], recv_sem=ask_recv.at[d],
            device_id={"rows": peer}, device_id_type=MESH,
        )

    for d in range(1, readers):
        ask(d).start()

    def shift(s):
        return pltpu.make_async_remote_copy(
            src_ref=history, dst_ref=source.at[s],
            send_sem=shift_send.at[s], recv_sem=shift_recv.at[s],
            device_id={"delay": lax.rem(bin_at + s, bins)}, device_id_type=MESH,
        )

    for s in range(1, min(steps, bins)):
        @pl.when(bin_at + s < bins)
        def _():
            shift(s).start()

    mine = pl.ds(pl.multiple_of(me * cap, cap), cap)
    ask_in[mine] = ask_out[mine]
    source[0] = history[...]

    here = lax.div(row_of((rows, n)), exc) == lane_of((rows, n))
    listing = slots[...].astype(F32)
    shape = (rows, total * exc)
    lanes = lane_of(shape).astype(F32)
    which = lax.rem(row_of((rows, 1)), exc).astype(F32)
    for l in range(listed):
        slot = jnp.sum(jnp.where(here, listing[l : l + 1], 0.0), axis=1, keepdims=True)
        target = slot * exc + which
        spots[l] = jnp.where(lanes == target, 1.0, 0.0).astype(BF16)

    for d in range(1, readers):
        asked(d).wait_recv()
    shape = (total * exc, total)
    spread = jnp.where(lax.div(row_of(shape), exc) == lane_of(shape), 1.0, 0.0).astype(F32)
    target = dot(spread, ask_in[...])
    shape = (total * exc, width)
    target = target * exc + lax.rem(row_of(shape), exc).astype(F32)
    for h in range(rows // width):
        lanes = (lane_of(shape) + h * width).astype(F32)
        picks[:, h * width : (h + 1) * width] = jnp.where(lanes == target, 1.0, 0.0).astype(BF16)

    def chosen(products):
        place = lax.div(row_of((16, width)), exc)
        kept = products[:, :width]
        for i in range(1, group):
            kept = jnp.where(place == i, products[:, i * width : (i + 1) * width], kept)
        return kept

    def swap(t, d):
        peer = lax.rem(me + d, readers)
        return pltpu.make_async_remote_copy(
            src_ref=sent.at[t, pl.ds(pl.multiple_of(peer * chunk, chunk), chunk)],
            dst_ref=got.at[t, pl.ds(pl.multiple_of(me * chunk, chunk), chunk)],
            send_sem=swap_send.at[t, d], recv_sem=swap_recv.at[t, d],
            device_id={"rows": peer}, device_id_type=MESH,
        )

    def swapped(t, d):
        peer = lax.rem(me + readers - d, readers)
        there = got.at[t, pl.ds(pl.multiple_of(peer * chunk, chunk), chunk)]
        return pltpu.make_async_remote_copy(
            src_ref=there, dst_ref=there,
            send_sem=swap_send.at[t, d], recv_sem=swap_recv.at[t, d],
            device_id={"rows": peer}, device_id_type=MESH,
        )

    def part(t, k):
        return pltpu.make_async_remote_copy(
            src_ref=part_out.at[t], dst_ref=part_in.at[t, k],
            send_sem=part_send.at[t], recv_sem=part_recv.at[t, k],
            device_id={"delay": 0}, device_id_type=MESH,
        )

    def tell(t, d):
        return pltpu.make_async_remote_copy(
            src_ref=driven.at[t], dst_ref=driven.at[t],
            send_sem=driven_send.at[t, d], recv_sem=driven_recv.at[t],
            device_id={"delay": d}, device_id_type=MESH,
        )

    def solve(u):
        later = jnp.minimum(u + 1 + bin_at, steps)

        def some(q, c):
            for i in range(4):
                g = q * 4 + i
                at = pl.ds(pl.multiple_of(g * 16, 16), 16)
                right = jnp.concatenate([diag[g * group + j] for j in range(group)], axis=1)
                value = chosen(dot(driven[u, at], right))
                out[u, at] = value
                source[later, at] = value.astype(BF16)
            return c

        lax.fori_loop(0, groups // 4, some, 0)

    def step(t, carry):
        @pl.when((t > 0) & (bin_at >= t))
        def _():
            pltpu.make_async_remote_copy(
                src_ref=history, dst_ref=source.at[t],
                send_sem=shift_send.at[t], recv_sem=shift_recv.at[t],
                device_id={"delay": lax.rem(bin_at + 1, bins)}, device_id_type=MESH,
            ).wait_recv()

        @pl.when((bin_at > 0) & (bin_at < t))
        def _():
            u = t - 1 - bin_at
            tell(u, 0).wait_recv()

            @pl.when(u == 0)
            def _():
                loads[2].wait()

            solve(u)

        sent[t] = dot(picks[...], source[t]).astype(BF16)
        for d in range(1, readers):
            swap(t, d).start()
        mine = pl.ds(pl.multiple_of(me * chunk, chunk), chunk)
        got[t, mine] = sent[t, mine]
        for d in range(1, readers):
            swapped(t, d).wait_recv()
        arrived = got[t]
        for l in range(listed):
            lhs[:, l * width : (l + 1) * width] = dot(spots[l], arrived).astype(BF16)

        @pl.when(t == 0)
        def _():
            loads[0].wait()
            loads[1].wait()

        def some(q, c):
            for i in range(4):
                g = q * 4 + i
                at = pl.ds(pl.multiple_of(g * 16, 16), 16)
                right = jnp.concatenate([tiles[g * group + j] for j in range(group)], axis=1)
                value = chosen(dot(lhs[at], right))
                part_out[t, at] = value.astype(BF16)
                part_own[at] = value
            return c

        lax.fori_loop(0, groups // 4, some, 0)

        @pl.when(bin_at > 0)
        def _():
            part(t, bin_at).start()

        @pl.when(bin_at == 0)
        def _():
            value = part_own[...]
            for k in range(1, bins):
                part(t, k).wait_recv()
                value = value + part_in[t, k].astype(F32)
            driven[t] = (excitation[t] - value).astype(BF16)
            for d in range(1, bins):
                tell(t, d).start()

            @pl.when(t == 0)
            def _():
                loads[2].wait()

            solve(t)

        return carry

    lax.fori_loop(0, steps, step, 0)

    @pl.when(bin_at > 0)
    def _():
        def last(u, c):
            @pl.when(u >= steps - 1 - bin_at)
            def _():
                tell(u, 0).wait_recv()

                @pl.when(u == 0)
                def _():
                    loads[2].wait()

                solve(u)
            return c

        lax.fori_loop(0, steps, last, 0)

    for d in range(1, readers):
        ask(d).wait_send()
    for s in range(1, min(steps, bins)):
        @pl.when(bin_at + s < bins)
        def _():
            shift(s).wait_send()

    def drain(t, c):
        for d in range(1, readers):
            swap(t, d).wait_send()

        @pl.when(bin_at > 0)
        def _():
            part(t, bin_at).wait_send()

        @pl.when(bin_at == 0)
        def _():
            for d in range(1, bins):
                tell(t, d).wait_send()
        return c

    lax.fori_loop(0, steps, drain, 0)


def body(retarded_tiles, wanted_blocks, tile_slots, diag_inverse, excitation, history_init):
    readers, bins = lax.axis_size("rows"), lax.axis_size("delay")
    _, n, listed, width, _ = retarded_tiles.shape
    steps, _, exc, _ = excitation.shape
    cap = wanted_blocks.shape[-1]
    rows, taken = n * exc, readers * cap * exc
    sizes = (readers, bins, steps, n, listed, exc, cap, width)
    vmem = pl.BlockSpec(memory_space=pltpu.VMEM)
    anywhere = pl.BlockSpec(memory_space=pltpu.HBM)
    dma = pltpu.SemaphoreType.DMA
    solved = pl.pallas_call(
        functools.partial(kernel, sizes),
        out_shape=jax.ShapeDtypeStruct((steps, rows, width), F32),
        in_specs=[vmem, vmem, vmem, anywhere, anywhere, anywhere],
        out_specs=vmem,
        scratch_shapes=[
            pltpu.VMEM((n, listed * width, width), BF16),
            pltpu.VMEM((n, width, width), BF16),
            pltpu.VMEM((steps, rows, width), F32),
            pltpu.VMEM((taken, rows), BF16),
            pltpu.VMEM((listed, rows, taken), BF16),
            pltpu.VMEM((readers * cap, width), F32),
            pltpu.VMEM((readers * cap, width), F32),
            pltpu.VMEM((steps + 1, rows, width), BF16),
            pltpu.VMEM((steps, taken, width), BF16),
            pltpu.VMEM((steps, taken, width), BF16),
            pltpu.VMEM((rows, listed * width), BF16),
            pltpu.VMEM((rows, width), F32),
            pltpu.VMEM((steps, rows, width), BF16),
            pltpu.VMEM((steps, bins, rows, width), BF16),
            pltpu.VMEM((steps, rows, width), BF16),
            dma((3,)),
            dma((readers,)),
            dma((readers,)),
            dma((steps,)),
            dma((steps,)),
            dma((steps, readers)),
            dma((steps, readers)),
            dma((steps,)),
            dma((steps, bins)),
            dma((steps, bins)),
            dma((steps,)),
        ],
        compiler_params=pltpu.CompilerParams(
            collective_id=0, has_side_effects=True, vmem_limit_bytes=44 << 20
        ),
        cost_estimate=pl.CostEstimate(
            flops=2 * steps * rows * width * width * (listed + 1), transcendentals=0,
            bytes_accessed=2 * n * width * width * (listed + 1),
        ),
    )(
        history_init.reshape(rows, width),
        wanted_blocks.reshape(readers, cap),
        tile_slots.reshape(n, listed).T,
        retarded_tiles.reshape(n, listed * width, width),
        diag_inverse,
        excitation.reshape(steps, rows, width),
    )
    return solved.reshape(steps, n, exc, width)


def solution(mesh):
    return jax.shard_map(
        body,
        mesh=mesh,
        in_specs=(
            P("delay", "rows", None, None, None),
            P("delay", "rows", None, None),
            P("delay", "rows", None),
            P("rows", None, None),
            P(None, "rows", None, None),
            P("delay", "rows", None, None),
        ),
        out_specs=P(None, "rows", None, None),
        check_vma=False,
    )
```

```python
import functools

import jax
import jax.numpy as jnp
from jax import lax
from jax.experimental import pallas as pl
from jax.experimental.pallas import tpu as pltpu
from jax.sharding import PartitionSpec as P

MESH = pl.DeviceIdType.MESH
F32 = jnp.float32
BF16 = jnp.bfloat16


def row_of(shape):
    return lax.broadcasted_iota(jnp.int32, shape, 0)


def lane_of(shape):
    return lax.broadcasted_iota(jnp.int32, shape, 1)


def dot(a, b):
    return jnp.dot(a, b, preferred_element_type=F32)


def kernel(
    sizes,
    history_hbm, wanted_hbm, slots_hbm, tiles_hbm, diag_hbm, excitation_hbm,
    out,
    wanted, slots, tiles, diag, excitation, picks, spots, ask_out, ask_in, source, sent, got, lhs,
    part_out, quarter_in, sum_out, sum_in, driven,
    load_sem, ask_send, ask_recv, shift_send, shift_recv, swap_send, swap_recv,
    part_send, part_recv, sum_send, sum_recv, driven_send, driven_recv,
):
    readers, bins, steps, n, listed, exc, cap, width = sizes
    me = lax.axis_index("rows")
    bin_at = lax.axis_index("delay")
    rows = n * exc
    chunk = cap * exc
    group = 16 // exc
    groups = rows // 16
    quarter = rows // bins

    loads = [
        pltpu.make_async_copy(excitation_hbm, excitation, load_sem.at[0]),
        pltpu.make_async_copy(tiles_hbm, tiles, load_sem.at[1]),
        pltpu.make_async_copy(diag_hbm, diag, load_sem.at[2]),
        pltpu.make_async_copy(wanted_hbm, wanted, load_sem.at[3]),
        pltpu.make_async_copy(slots_hbm, slots, load_sem.at[4]),
        pltpu.make_async_copy(history_hbm, source.at[0], load_sem.at[5]),
    ]
    for i in (3, 4, 5, 1, 0, 2):
        loads[i].start()

    barrier = pltpu.get_barrier_semaphore()
    for d in range(1, readers):
        pl.semaphore_signal(barrier, inc=1, device_id={"rows": lax.rem(me + d, readers)}, device_id_type=MESH)
    for d in range(1, bins):
        pl.semaphore_signal(barrier, inc=1, device_id={"delay": lax.rem(bin_at + d, bins)}, device_id_type=MESH)

    total = readers * cap
    shape = (total, readers)
    spread = jnp.where(lax.div(row_of(shape), cap) == lane_of(shape), 1.0, 0.0).astype(F32)
    loads[3].wait()
    every = dot(spread, wanted[...].astype(F32))
    shape = (total, cap)
    own = jnp.where(lax.rem(row_of(shape), cap) == lane_of(shape), every, 0.0)
    ask_out[...] = jnp.broadcast_to(jnp.sum(own, axis=1, keepdims=True), (total, width))

    pl.semaphore_wait(barrier, readers - 1 + bins - 1)

    def ask(d):
        peer = lax.rem(me + d, readers)
        return pltpu.make_async_remote_copy(
            src_ref=ask_out.at[pl.ds(pl.multiple_of(peer * cap, cap), cap)],
            dst_ref=ask_in.at[pl.ds(pl.multiple_of(me * cap, cap), cap)],
            send_sem=ask_send.at[d], recv_sem=ask_recv.at[d],
            device_id={"rows": peer}, device_id_type=MESH,
        )

    def asked(d):
        peer = lax.rem(me + readers - d, readers)
        there = ask_in.at[pl.ds(pl.multiple_of(peer * cap, cap), cap)]
        return pltpu.make_async_remote_copy(
            src_ref=there, dst_ref=there,
            send_sem=ask_send.at[d], recv_sem=ask_recv.at[d],
            device_id={"rows": peer}, device_id_type=MESH,
        )

    for d in range(1, readers):
        ask(d).start()

    def shift(s):
        return pltpu.make_async_remote_copy(
            src_ref=source.at[0], dst_ref=source.at[s],
            send_sem=shift_send.at[s], recv_sem=shift_recv.at[s],
            device_id={"delay": lax.rem(bin_at + s, bins)}, device_id_type=MESH,
        )

    loads[5].wait()
    for s in range(1, min(steps, bins)):
        @pl.when(bin_at + s < bins)
        def _():
            shift(s).start()

    mine = pl.ds(pl.multiple_of(me * cap, cap), cap)
    ask_in[mine] = ask_out[mine]

    here = lax.div(row_of((rows, n)), exc) == lane_of((rows, n))
    loads[4].wait()
    listing = slots[...].astype(F32)
    shape = (rows, total * exc)
    lanes = lane_of(shape).astype(F32)
    which = lax.rem(row_of((rows, 1)), exc).astype(F32)
    for l in range(listed):
        slot = jnp.sum(jnp.where(here, listing[l : l + 1], 0.0), axis=1, keepdims=True)
        target = slot * exc + which
        spots[l] = jnp.where(lanes == target, 1.0, 0.0).astype(BF16)

    for d in range(1, readers):
        asked(d).wait_recv()
    shape = (total * exc, total)
    spread = jnp.where(lax.div(row_of(shape), exc) == lane_of(shape), 1.0, 0.0).astype(F32)
    target = dot(spread, ask_in[...])
    shape = (total * exc, width)
    target = target * exc + lax.rem(row_of(shape), exc).astype(F32)
    for h in range(rows // width):
        lanes = (lane_of(shape) + h * width).astype(F32)
        picks[:, h * width : (h + 1) * width] = jnp.where(lanes == target, 1.0, 0.0).astype(BF16)

    def chosen(products):
        place = lax.div(row_of((16, width)), exc)
        kept = products[:, :width]
        for i in range(1, group):
            kept = jnp.where(place == i, products[:, i * width : (i + 1) * width], kept)
        return kept

    def swap(t, d):
        peer = lax.rem(me + d, readers)
        return pltpu.make_async_remote_copy(
            src_ref=sent.at[t, pl.ds(pl.multiple_of(peer * chunk, chunk), chunk)],
            dst_ref=got.at[t, pl.ds(pl.multiple_of(me * chunk, chunk), chunk)],
            send_sem=swap_send.at[t, d], recv_sem=swap_recv.at[t, d],
            device_id={"rows": peer}, device_id_type=MESH,
        )

    def swapped(t, d):
        peer = lax.rem(me + readers - d, readers)
        there = got.at[t, pl.ds(pl.multiple_of(peer * chunk, chunk), chunk)]
        return pltpu.make_async_remote_copy(
            src_ref=there, dst_ref=there,
            send_sem=swap_send.at[t, d], recv_sem=swap_recv.at[t, d],
            device_id={"rows": peer}, device_id_type=MESH,
        )

    def at_quarter(k):
        return pl.ds(pl.multiple_of(k * quarter, quarter), quarter)

    def part(t, d):
        peer = lax.rem(bin_at + d, bins)
        return pltpu.make_async_remote_copy(
            src_ref=part_out.at[t, at_quarter(peer)], dst_ref=quarter_in.at[t, bin_at],
            send_sem=part_send.at[t, d], recv_sem=part_recv.at[t, d],
            device_id={"delay": peer}, device_id_type=MESH,
        )

    def parted(t, d):
        peer = lax.rem(bin_at + bins - d, bins)
        there = quarter_in.at[t, peer]
        return pltpu.make_async_remote_copy(
            src_ref=there, dst_ref=there,
            send_sem=part_send.at[t, d], recv_sem=part_recv.at[t, d],
            device_id={"delay": peer}, device_id_type=MESH,
        )

    def summed(t, k):
        return pltpu.make_async_remote_copy(
            src_ref=sum_out.at[t], dst_ref=sum_in.at[t, k],
            send_sem=sum_send.at[t], recv_sem=sum_recv.at[t, k],
            device_id={"delay": 0}, device_id_type=MESH,
        )

    def tell(t, d):
        return pltpu.make_async_remote_copy(
            src_ref=driven.at[t], dst_ref=driven.at[t],
            send_sem=driven_send.at[t, d], recv_sem=driven_recv.at[t],
            device_id={"delay": d}, device_id_type=MESH,
        )

    def solve(u):
        later = jnp.minimum(u + 1 + bin_at, steps)

        def some(q, c):
            for i in range(4):
                g = q * 4 + i
                at = pl.ds(pl.multiple_of(g * 16, 16), 16)
                right = jnp.concatenate([diag[g * group + j] for j in range(group)], axis=1)
                value = chosen(dot(driven[u, at], right))
                out[u, at] = value
                source[later, at] = value.astype(BF16)
            return c

        lax.fori_loop(0, groups // 4, some, 0)

    def step(t, carry):
        @pl.when((t > 0) & (bin_at >= t))
        def _():
            pltpu.make_async_remote_copy(
                src_ref=source.at[0], dst_ref=source.at[t],
                send_sem=shift_send.at[t], recv_sem=shift_recv.at[t],
                device_id={"delay": lax.rem(bin_at + 1, bins)}, device_id_type=MESH,
            ).wait_recv()

        @pl.when((bin_at > 0) & (bin_at < t))
        def _():
            u = t - 1 - bin_at
            tell(u, 0).wait_recv()

            @pl.when(u == 0)
            def _():
                loads[2].wait()

            solve(u)

        sent[t] = dot(picks[...], source[t]).astype(BF16)
        for d in range(1, readers):
            swap(t, d).start()
        mine = pl.ds(pl.multiple_of(me * chunk, chunk), chunk)
        got[t, mine] = sent[t, mine]
        for d in range(1, readers):
            swapped(t, d).wait_recv()
        arrived = got[t]
        for l in range(listed):
            lhs[:, l * width : (l + 1) * width] = dot(spots[l], arrived).astype(BF16)

        @pl.when(t == 0)
        def _():
            loads[0].wait()
            loads[1].wait()

        def some(q, c):
            for i in range(4):
                g = q * 4 + i
                at = pl.ds(pl.multiple_of(g * 16, 16), 16)
                right = jnp.concatenate([tiles[g * group + j] for j in range(group)], axis=1)
                value = chosen(dot(lhs[at], right))
                part_out[t, at] = value
            return c

        lax.fori_loop(0, groups // 4, some, 0)

        @pl.when(bin_at > 0)
        def _():
            for d in range(1, bins):
                part(t, d).start()
            sum_out[t] = part_out[t, at_quarter(bin_at)]
            for d in range(1, bins):
                @pl.when(lax.rem(bin_at + bins - d, bins) > 0)
                def _():
                    parted(t, d).wait_recv()
                    sum_out[t] += quarter_in[t, lax.rem(bin_at + bins - d, bins)]
            summed(t, bin_at).start()

        @pl.when(bin_at == 0)
        def _():
            value = part_out[t, :quarter]
            for d in range(1, bins):
                parted(t, d).wait_recv()
                value = value + quarter_in[t, bins - d]
            driven[t, :quarter] = (excitation[t, :quarter] - value).astype(BF16)
            for k in range(1, bins):
                here = slice(k * quarter, (k + 1) * quarter)
                summed(t, k).wait_recv()
                value = part_out[t, here] + sum_in[t, k]
                driven[t, here] = (excitation[t, here] - value).astype(BF16)
            for d in range(1, bins):
                tell(t, d).start()

            @pl.when(t == 0)
            def _():
                loads[2].wait()

            solve(t)

        return carry

    lax.fori_loop(0, steps, step, 0)

    @pl.when(bin_at > 0)
    def _():
        def last(u, c):
            @pl.when(u >= steps - 1 - bin_at)
            def _():
                tell(u, 0).wait_recv()

                @pl.when(u == 0)
                def _():
                    loads[2].wait()

                solve(u)
            return c

        lax.fori_loop(0, steps, last, 0)

    for d in range(1, readers):
        ask(d).wait_send()
    for s in range(1, min(steps, bins)):
        @pl.when(bin_at + s < bins)
        def _():
            shift(s).wait_send()

    def drain(t, c):
        for d in range(1, readers):
            swap(t, d).wait_send()

        @pl.when(bin_at > 0)
        def _():
            for d in range(1, bins):
                part(t, d).wait_send()
            summed(t, bin_at).wait_send()

        @pl.when(bin_at == 0)
        def _():
            for d in range(1, bins):
                tell(t, d).wait_send()
        return c

    lax.fori_loop(0, steps, drain, 0)


def body(retarded_tiles, wanted_blocks, tile_slots, diag_inverse, excitation, history_init):
    readers, bins = lax.axis_size("rows"), lax.axis_size("delay")
    _, n, listed, width, _ = retarded_tiles.shape
    steps, _, exc, _ = excitation.shape
    cap = wanted_blocks.shape[-1]
    rows, taken = n * exc, readers * cap * exc
    sizes = (readers, bins, steps, n, listed, exc, cap, width)
    vmem = pl.BlockSpec(memory_space=pltpu.VMEM)
    anywhere = pl.BlockSpec(memory_space=pltpu.HBM)
    dma = pltpu.SemaphoreType.DMA
    solved = pl.pallas_call(
        functools.partial(kernel, sizes),
        out_shape=pltpu.VMEM((steps, rows, width), F32),
        in_specs=[anywhere] * 6,
        out_specs=vmem,
        scratch_shapes=[
            pltpu.VMEM((readers, cap), jnp.int32),
            pltpu.VMEM((listed, n), jnp.int32),
            pltpu.VMEM((n, listed * width, width), BF16),
            pltpu.VMEM((n, width, width), BF16),
            pltpu.VMEM((steps, rows, width), F32),
            pltpu.VMEM((taken, rows), BF16),
            pltpu.VMEM((listed, rows, taken), BF16),
            pltpu.VMEM((readers * cap, width), F32),
            pltpu.VMEM((readers * cap, width), F32),
            pltpu.VMEM((steps + 1, rows, width), BF16),
            pltpu.VMEM((steps, taken, width), BF16),
            pltpu.VMEM((steps, taken, width), BF16),
            pltpu.VMEM((rows, listed * width), BF16),
            pltpu.VMEM((steps, rows, width), F32),
            pltpu.VMEM((steps, bins, rows // bins, width), F32),
            pltpu.VMEM((steps, rows // bins, width), F32),
            pltpu.VMEM((steps, bins, rows // bins, width), F32),
            pltpu.VMEM((steps, rows, width), BF16),
            dma((6,)),
            dma((readers,)),
            dma((readers,)),
            dma((steps,)),
            dma((steps,)),
            dma((steps, readers)),
            dma((steps, readers)),
            dma((steps, bins)),
            dma((steps, bins)),
            dma((steps,)),
            dma((steps, bins)),
            dma((steps, bins)),
            dma((steps,)),
        ],
        compiler_params=pltpu.CompilerParams(
            collective_id=0, has_side_effects=True, vmem_limit_bytes=57 << 20
        ),
        cost_estimate=pl.CostEstimate(
            flops=2 * steps * rows * width * width * (listed + 1), transcendentals=0,
            bytes_accessed=2 * n * width * width * (listed + 1),
        ),
    )(
        history_init.reshape(rows, width),
        wanted_blocks.reshape(readers, cap),
        tile_slots.reshape(n, listed).T,
        retarded_tiles.reshape(n, listed * width, width),
        diag_inverse,
        excitation.reshape(steps, rows, width),
    )
    return solved.reshape(steps, n, exc, width)


def solution(mesh):
    return jax.shard_map(
        body,
        mesh=mesh,
        in_specs=(
            P("delay", "rows", None, None, None),
            P("delay", "rows", None, None),
            P("delay", "rows", None),
            P("rows", None, None),
            P(None, "rows", None, None),
            P("delay", "rows", None, None),
        ),
        out_specs=P(None, "rows", None, None),
        check_vma=False,
    )
```

```python
import functools

import jax
import jax.numpy as jnp
from jax import lax
from jax.experimental import pallas as pl
from jax.experimental.pallas import tpu as pltpu
from jax.sharding import PartitionSpec as P

MESH = pl.DeviceIdType.MESH
F32 = jnp.float32
BF16 = jnp.bfloat16


def row_of(shape):
    return lax.broadcasted_iota(jnp.int32, shape, 0)


def lane_of(shape):
    return lax.broadcasted_iota(jnp.int32, shape, 1)


def dot(a, b):
    return jnp.dot(a, b, preferred_element_type=F32)


def kernel(
    sizes,
    history_hbm, wanted_hbm, slots_hbm, tiles_hbm, diag_hbm, excitation_hbm,
    out,
    wanted, slots, tiles, diag, excitation, picks, spots, ask_out, ask_in, source, sent, got, lhs,
    part_out, part_in, driven,
    load_sem, ask_send, ask_recv, shift_send, shift_recv, swap_send, swap_recv,
    part_send, part_recv, driven_send, driven_recv,
):
    readers, bins, steps, n, listed, exc, cap, width = sizes
    me = lax.axis_index("rows")
    bin_at = lax.axis_index("delay")
    rows = n * exc
    chunk = cap * exc
    group = 16 // exc
    groups = rows // 16

    loads = [
        pltpu.make_async_copy(excitation_hbm, excitation, load_sem.at[0]),
        pltpu.make_async_copy(tiles_hbm, tiles, load_sem.at[1]),
        pltpu.make_async_copy(diag_hbm, diag, load_sem.at[2]),
        pltpu.make_async_copy(wanted_hbm, wanted, load_sem.at[3]),
        pltpu.make_async_copy(slots_hbm, slots, load_sem.at[4]),
        pltpu.make_async_copy(history_hbm, source.at[0], load_sem.at[5]),
    ]
    for i in (3, 4, 5, 1, 0, 2):
        loads[i].start()

    barrier = pltpu.get_barrier_semaphore()
    for d in range(1, readers):
        pl.semaphore_signal(barrier, inc=1, device_id={"rows": lax.rem(me + d, readers)}, device_id_type=MESH)
    for d in range(1, bins):
        pl.semaphore_signal(barrier, inc=1, device_id={"delay": lax.rem(bin_at + d, bins)}, device_id_type=MESH)

    total = readers * cap
    shape = (total, readers)
    spread = jnp.where(lax.div(row_of(shape), cap) == lane_of(shape), 1.0, 0.0).astype(F32)
    loads[3].wait()
    every = dot(spread, wanted[...].astype(F32))
    shape = (total, cap)
    own = jnp.where(lax.rem(row_of(shape), cap) == lane_of(shape), every, 0.0)
    ask_out[...] = jnp.broadcast_to(jnp.sum(own, axis=1, keepdims=True), (total, width))

    pl.semaphore_wait(barrier, readers - 1 + bins - 1)

    def ask(d):
        peer = lax.rem(me + d, readers)
        return pltpu.make_async_remote_copy(
            src_ref=ask_out.at[pl.ds(pl.multiple_of(peer * cap, cap), cap)],
            dst_ref=ask_in.at[pl.ds(pl.multiple_of(me * cap, cap), cap)],
            send_sem=ask_send.at[d], recv_sem=ask_recv.at[d],
            device_id={"rows": peer}, device_id_type=MESH,
        )

    def asked(d):
        peer = lax.rem(me + readers - d, readers)
        there = ask_in.at[pl.ds(pl.multiple_of(peer * cap, cap), cap)]
        return pltpu.make_async_remote_copy(
            src_ref=there, dst_ref=there,
            send_sem=ask_send.at[d], recv_sem=ask_recv.at[d],
            device_id={"rows": peer}, device_id_type=MESH,
        )

    for d in range(1, readers):
        ask(d).start()

    def shift(s):
        return pltpu.make_async_remote_copy(
            src_ref=source.at[0], dst_ref=source.at[s],
            send_sem=shift_send.at[s], recv_sem=shift_recv.at[s],
            device_id={"delay": lax.rem(bin_at + s, bins)}, device_id_type=MESH,
        )

    loads[5].wait()
    for s in range(1, min(steps, bins)):
        @pl.when(bin_at + s < bins)
        def _():
            shift(s).start()

    mine = pl.ds(pl.multiple_of(me * cap, cap), cap)
    ask_in[mine] = ask_out[mine]

    here = lax.div(row_of((rows, n)), exc) == lane_of((rows, n))
    loads[4].wait()
    listing = slots[...].astype(F32)
    shape = (rows, total * exc)
    lanes = lane_of(shape).astype(F32)
    which = lax.rem(row_of((rows, 1)), exc).astype(F32)
    for l in range(listed):
        slot = jnp.sum(jnp.where(here, listing[l : l + 1], 0.0), axis=1, keepdims=True)
        target = slot * exc + which
        spots[l] = jnp.where(lanes == target, 1.0, 0.0).astype(BF16)

    for d in range(1, readers):
        asked(d).wait_recv()
    shape = (total * exc, total)
    spread = jnp.where(lax.div(row_of(shape), exc) == lane_of(shape), 1.0, 0.0).astype(F32)
    target = dot(spread, ask_in[...])
    shape = (total * exc, width)
    target = target * exc + lax.rem(row_of(shape), exc).astype(F32)
    for h in range(rows // width):
        lanes = (lane_of(shape) + h * width).astype(F32)
        picks[:, h * width : (h + 1) * width] = jnp.where(lanes == target, 1.0, 0.0).astype(BF16)

    def chosen(products):
        place = lax.div(row_of((16, width)), exc)
        kept = products[:, :width]
        for i in range(1, group):
            kept = jnp.where(place == i, products[:, i * width : (i + 1) * width], kept)
        return kept

    def swap(t, d):
        peer = lax.rem(me + d, readers)
        return pltpu.make_async_remote_copy(
            src_ref=sent.at[t, pl.ds(pl.multiple_of(peer * chunk, chunk), chunk)],
            dst_ref=got.at[t, pl.ds(pl.multiple_of(me * chunk, chunk), chunk)],
            send_sem=swap_send.at[t, d], recv_sem=swap_recv.at[t, d],
            device_id={"rows": peer}, device_id_type=MESH,
        )

    def swapped(t, d):
        peer = lax.rem(me + readers - d, readers)
        there = got.at[t, pl.ds(pl.multiple_of(peer * chunk, chunk), chunk)]
        return pltpu.make_async_remote_copy(
            src_ref=there, dst_ref=there,
            send_sem=swap_send.at[t, d], recv_sem=swap_recv.at[t, d],
            device_id={"rows": peer}, device_id_type=MESH,
        )

    def part(t, k):
        return pltpu.make_async_remote_copy(
            src_ref=part_out.at[t], dst_ref=part_in.at[t, k],
            send_sem=part_send.at[t], recv_sem=part_recv.at[t, k],
            device_id={"delay": 0}, device_id_type=MESH,
        )

    def tell(t, d):
        return pltpu.make_async_remote_copy(
            src_ref=driven.at[t], dst_ref=driven.at[t],
            send_sem=driven_send.at[t, d], recv_sem=driven_recv.at[t],
            device_id={"delay": d}, device_id_type=MESH,
        )

    def solve(u):
        later = jnp.minimum(u + 1 + bin_at, steps)

        def some(q, c):
            for i in range(4):
                g = q * 4 + i
                at = pl.ds(pl.multiple_of(g * 16, 16), 16)
                right = jnp.concatenate([diag[g * group + j] for j in range(group)], axis=1)
                value = chosen(dot(driven[u, at], right))
                out[u, at] = value
                source[later, at] = value.astype(BF16)
            return c

        lax.fori_loop(0, groups // 4, some, 0)

    def launch(t):
        sent[t] = dot(picks[...], source[t]).astype(BF16)
        for d in range(1, readers):
            swap(t, d).start()
        mine = pl.ds(pl.multiple_of(me * chunk, chunk), chunk)
        got[t, mine] = sent[t, mine]

    def early(s, c):
        @pl.when(bin_at >= s)
        def _():
            pltpu.make_async_remote_copy(
                src_ref=source.at[0], dst_ref=source.at[s],
                send_sem=shift_send.at[s], recv_sem=shift_recv.at[s],
                device_id={"delay": lax.rem(bin_at + 1, bins)}, device_id_type=MESH,
            ).wait_recv()
            launch(s)
        return c

    launch(0)
    lax.fori_loop(1, steps, early, 0)

    def step(t, carry):
        @pl.when((bin_at > 0) & (bin_at < t))
        def _():
            u = t - 1 - bin_at
            tell(u, 0).wait_recv()

            @pl.when(u == 0)
            def _():
                loads[2].wait()

            solve(u)

        @pl.when(bin_at < t)
        def _():
            launch(t)

        for d in range(1, readers):
            swapped(t, d).wait_recv()
        arrived = got[t]
        for l in range(listed):
            lhs[:, l * width : (l + 1) * width] = dot(spots[l], arrived).astype(BF16)

        @pl.when(t == 0)
        def _():
            loads[0].wait()
            loads[1].wait()

        def some(q, c):
            for i in range(4):
                g = q * 4 + i
                at = pl.ds(pl.multiple_of(g * 16, 16), 16)
                right = jnp.concatenate([tiles[g * group + j] for j in range(group)], axis=1)
                value = chosen(dot(lhs[at], right))
                part_out[t, at] = value
            return c

        lax.fori_loop(0, groups // 4, some, 0)

        @pl.when(bin_at > 0)
        def _():
            part(t, bin_at).start()

        @pl.when(bin_at == 0)
        def _():
            value = part_out[t]
            for k in range(1, bins):
                part(t, k).wait_recv()
                value = value + part_in[t, k]
            driven[t] = (excitation[t] - value).astype(BF16)
            for d in range(1, bins):
                tell(t, d).start()

            @pl.when(t == 0)
            def _():
                loads[2].wait()

            solve(t)

        return carry

    lax.fori_loop(0, steps, step, 0)

    @pl.when(bin_at > 0)
    def _():
        def last(u, c):
            @pl.when(u >= steps - 1 - bin_at)
            def _():
                tell(u, 0).wait_recv()

                @pl.when(u == 0)
                def _():
                    loads[2].wait()

                solve(u)
            return c

        lax.fori_loop(0, steps, last, 0)

    for d in range(1, readers):
        ask(d).wait_send()
    for s in range(1, min(steps, bins)):
        @pl.when(bin_at + s < bins)
        def _():
            shift(s).wait_send()

    def drain(t, c):
        for d in range(1, readers):
            swap(t, d).wait_send()

        @pl.when(bin_at > 0)
        def _():
            part(t, bin_at).wait_send()

        @pl.when(bin_at == 0)
        def _():
            for d in range(1, bins):
                tell(t, d).wait_send()
        return c

    lax.fori_loop(0, steps, drain, 0)


def body(retarded_tiles, wanted_blocks, tile_slots, diag_inverse, excitation, history_init):
    readers, bins = lax.axis_size("rows"), lax.axis_size("delay")
    _, n, listed, width, _ = retarded_tiles.shape
    steps, _, exc, _ = excitation.shape
    cap = wanted_blocks.shape[-1]
    rows, taken = n * exc, readers * cap * exc
    sizes = (readers, bins, steps, n, listed, exc, cap, width)
    vmem = pl.BlockSpec(memory_space=pltpu.VMEM)
    anywhere = pl.BlockSpec(memory_space=pltpu.HBM)
    dma = pltpu.SemaphoreType.DMA
    solved = pl.pallas_call(
        functools.partial(kernel, sizes),
        out_shape=pltpu.VMEM((steps, rows, width), F32),
        in_specs=[anywhere] * 6,
        out_specs=vmem,
        scratch_shapes=[
            pltpu.VMEM((readers, cap), jnp.int32),
            pltpu.VMEM((listed, n), jnp.int32),
            pltpu.VMEM((n, listed * width, width), BF16),
            pltpu.VMEM((n, width, width), BF16),
            pltpu.VMEM((steps, rows, width), F32),
            pltpu.VMEM((taken, rows), BF16),
            pltpu.VMEM((listed, rows, taken), BF16),
            pltpu.VMEM((readers * cap, width), F32),
            pltpu.VMEM((readers * cap, width), F32),
            pltpu.VMEM((steps + 1, rows, width), BF16),
            pltpu.VMEM((steps, taken, width), BF16),
            pltpu.VMEM((steps, taken, width), BF16),
            pltpu.VMEM((rows, listed * width), BF16),
            pltpu.VMEM((steps, rows, width), F32),
            pltpu.VMEM((steps, bins, rows, width), F32),
            pltpu.VMEM((steps, rows, width), BF16),
            dma((6,)),
            dma((readers,)),
            dma((readers,)),
            dma((steps,)),
            dma((steps,)),
            dma((steps, readers)),
            dma((steps, readers)),
            dma((steps,)),
            dma((steps, bins)),
            dma((steps, bins)),
            dma((steps,)),
        ],
        compiler_params=pltpu.CompilerParams(
            collective_id=0, has_side_effects=True, vmem_limit_bytes=57 << 20
        ),
        cost_estimate=pl.CostEstimate(
            flops=2 * steps * rows * width * width * (listed + 1), transcendentals=0,
            bytes_accessed=2 * n * width * width * (listed + 1),
        ),
    )(
        history_init.reshape(rows, width),
        wanted_blocks.reshape(readers, cap),
        tile_slots.reshape(n, listed).T,
        retarded_tiles.reshape(n, listed * width, width),
        diag_inverse,
        excitation.reshape(steps, rows, width),
    )
    return solved.reshape(steps, n, exc, width)


def solution(mesh):
    return jax.shard_map(
        body,
        mesh=mesh,
        in_specs=(
            P("delay", "rows", None, None, None),
            P("delay", "rows", None, None),
            P("delay", "rows", None),
            P("rows", None, None),
            P(None, "rows", None, None),
            P("delay", "rows", None, None),
        ),
        out_specs=P(None, "rows", None, None),
        check_vma=False,
    )
```

```python
import functools

import jax
import jax.numpy as jnp
from jax import lax
from jax.experimental import pallas as pl
from jax.experimental.pallas import tpu as pltpu
from jax.sharding import PartitionSpec as P

MESH = pl.DeviceIdType.MESH
F32 = jnp.float32
BF16 = jnp.bfloat16


def row_of(shape):
    return lax.broadcasted_iota(jnp.int32, shape, 0)


def lane_of(shape):
    return lax.broadcasted_iota(jnp.int32, shape, 1)


def dot(a, b):
    return jnp.dot(a, b, preferred_element_type=F32)


def kernel(
    sizes,
    history_hbm, wanted_hbm, slots_hbm, tiles_hbm, diag_hbm, excitation_hbm,
    out,
    wanted, slots, tiles, diag, excitation, picks, spots, ask_out, ask_in, source, sent, got, lhs,
    part_out, part_in, driven,
    load_sem, ask_send, ask_recv, shift_send, shift_recv, swap_send, swap_recv,
    part_send, part_recv, driven_send, driven_recv,
):
    readers, bins, steps, n, listed, exc, cap, width = sizes
    me = lax.axis_index("rows")
    bin_at = lax.axis_index("delay")
    rows = n * exc
    chunk = cap * exc
    group = 16 // exc
    groups = rows // 16

    loads = [
        pltpu.make_async_copy(excitation_hbm, excitation, load_sem.at[0]),
        pltpu.make_async_copy(tiles_hbm, tiles, load_sem.at[1]),
        pltpu.make_async_copy(diag_hbm, diag, load_sem.at[2]),
        pltpu.make_async_copy(wanted_hbm, wanted, load_sem.at[3]),
        pltpu.make_async_copy(slots_hbm, slots, load_sem.at[4]),
        pltpu.make_async_copy(history_hbm, source.at[0], load_sem.at[5]),
    ]
    for i in (3, 4, 5, 1, 0, 2):
        loads[i].start()

    barrier = pltpu.get_barrier_semaphore()
    for d in range(1, readers):
        pl.semaphore_signal(barrier, inc=1, device_id={"rows": lax.rem(me + d, readers)}, device_id_type=MESH)
    for d in range(1, bins):
        pl.semaphore_signal(barrier, inc=1, device_id={"delay": lax.rem(bin_at + d, bins)}, device_id_type=MESH)

    total = readers * cap
    shape = (total, readers)
    spread = jnp.where(lax.div(row_of(shape), cap) == lane_of(shape), 1.0, 0.0).astype(F32)
    loads[3].wait()
    every = dot(spread, wanted[...].astype(F32))
    shape = (total, cap)
    own = jnp.where(lax.rem(row_of(shape), cap) == lane_of(shape), every, 0.0)
    ask_out[...] = jnp.broadcast_to(jnp.sum(own, axis=1, keepdims=True), (total, width))

    pl.semaphore_wait(barrier, readers - 1 + bins - 1)

    def ask(d):
        peer = lax.rem(me + d, readers)
        return pltpu.make_async_remote_copy(
            src_ref=ask_out.at[pl.ds(pl.multiple_of(peer * cap, cap), cap)],
            dst_ref=ask_in.at[pl.ds(pl.multiple_of(me * cap, cap), cap)],
            send_sem=ask_send.at[d], recv_sem=ask_recv.at[d],
            device_id={"rows": peer}, device_id_type=MESH,
        )

    def asked(d):
        peer = lax.rem(me + readers - d, readers)
        there = ask_in.at[pl.ds(pl.multiple_of(peer * cap, cap), cap)]
        return pltpu.make_async_remote_copy(
            src_ref=there, dst_ref=there,
            send_sem=ask_send.at[d], recv_sem=ask_recv.at[d],
            device_id={"rows": peer}, device_id_type=MESH,
        )

    for d in range(1, readers):
        ask(d).start()

    def shift(s):
        return pltpu.make_async_remote_copy(
            src_ref=source.at[0], dst_ref=source.at[s],
            send_sem=shift_send.at[s], recv_sem=shift_recv.at[s],
            device_id={"delay": lax.rem(bin_at + s, bins)}, device_id_type=MESH,
        )

    loads[5].wait()
    for s in range(1, min(steps, bins)):
        @pl.when(bin_at + s < bins)
        def _():
            shift(s).start()

    mine = pl.ds(pl.multiple_of(me * cap, cap), cap)
    ask_in[mine] = ask_out[mine]

    here = lax.div(row_of((rows, n)), exc) == lane_of((rows, n))
    loads[4].wait()
    listing = slots[...].astype(F32)
    shape = (rows, total * exc)
    lanes = lane_of(shape).astype(F32)
    which = lax.rem(row_of((rows, 1)), exc).astype(F32)
    for l in range(listed):
        slot = jnp.sum(jnp.where(here, listing[l : l + 1], 0.0), axis=1, keepdims=True)
        target = slot * exc + which
        spots[l] = jnp.where(lanes == target, 1.0, 0.0).astype(BF16)

    for d in range(1, readers):
        asked(d).wait_recv()
    shape = (total * exc, total)
    spread = jnp.where(lax.div(row_of(shape), exc) == lane_of(shape), 1.0, 0.0).astype(F32)
    target = dot(spread, ask_in[...])
    shape = (total * exc, width)
    target = target * exc + lax.rem(row_of(shape), exc).astype(F32)
    for h in range(rows // width):
        lanes = (lane_of(shape) + h * width).astype(F32)
        picks[:, h * width : (h + 1) * width] = jnp.where(lanes == target, 1.0, 0.0).astype(BF16)

    def chosen(products):
        place = lax.div(row_of((16, width)), exc)
        kept = products[:, :width]
        for i in range(1, group):
            kept = jnp.where(place == i, products[:, i * width : (i + 1) * width], kept)
        return kept

    def swap(t, d):
        peer = lax.rem(me + d, readers)
        return pltpu.make_async_remote_copy(
            src_ref=sent.at[t, pl.ds(pl.multiple_of(peer * chunk, chunk), chunk)],
            dst_ref=got.at[t, pl.ds(pl.multiple_of(me * chunk, chunk), chunk)],
            send_sem=swap_send.at[t, d], recv_sem=swap_recv.at[t, d],
            device_id={"rows": peer}, device_id_type=MESH,
        )

    def swapped(t, d):
        peer = lax.rem(me + readers - d, readers)
        there = got.at[t, pl.ds(pl.multiple_of(peer * chunk, chunk), chunk)]
        return pltpu.make_async_remote_copy(
            src_ref=there, dst_ref=there,
            send_sem=swap_send.at[t, d], recv_sem=swap_recv.at[t, d],
            device_id={"rows": peer}, device_id_type=MESH,
        )

    def part(t, k):
        return pltpu.make_async_remote_copy(
            src_ref=part_out.at[t], dst_ref=part_in.at[t, k],
            send_sem=part_send.at[t], recv_sem=part_recv.at[t, k],
            device_id={"delay": jnp.where(bin_at == 1, 0, lax.rem(bin_at, 2))}, device_id_type=MESH,
        )

    def tell(t, d):
        return pltpu.make_async_remote_copy(
            src_ref=driven.at[t], dst_ref=driven.at[t],
            send_sem=driven_send.at[t, d], recv_sem=driven_recv.at[t],
            device_id={"delay": d}, device_id_type=MESH,
        )

    def solve(u):
        later = jnp.minimum(u + 1 + bin_at, steps)

        def some(q, c):
            for i in range(4):
                g = q * 4 + i
                at = pl.ds(pl.multiple_of(g * 16, 16), 16)
                right = jnp.concatenate([diag[g * group + j] for j in range(group)], axis=1)
                value = chosen(dot(driven[u, at], right))
                out[u, at] = value
                source[later, at] = value.astype(BF16)
            return c

        lax.fori_loop(0, groups // 4, some, 0)

    def launch(t):
        sent[t] = dot(picks[...], source[t]).astype(BF16)
        for d in range(1, readers):
            swap(t, d).start()
        mine = pl.ds(pl.multiple_of(me * chunk, chunk), chunk)
        got[t, mine] = sent[t, mine]

    def early(s, c):
        @pl.when(bin_at >= s)
        def _():
            pltpu.make_async_remote_copy(
                src_ref=source.at[0], dst_ref=source.at[s],
                send_sem=shift_send.at[s], recv_sem=shift_recv.at[s],
                device_id={"delay": lax.rem(bin_at + 1, bins)}, device_id_type=MESH,
            ).wait_recv()
            launch(s)
        return c

    launch(0)
    lax.fori_loop(1, steps, early, 0)

    def step(t, carry):
        @pl.when((bin_at > 0) & (bin_at < t))
        def _():
            u = t - 1 - bin_at
            tell(u, 0).wait_recv()

            @pl.when(u == 0)
            def _():
                loads[2].wait()

            solve(u)

        @pl.when(bin_at < t)
        def _():
            launch(t)

        for d in range(1, readers):
            swapped(t, d).wait_recv()
        arrived = got[t]
        for l in range(listed):
            lhs[:, l * width : (l + 1) * width] = dot(spots[l], arrived).astype(BF16)

        @pl.when(t == 0)
        def _():
            loads[0].wait()
            loads[1].wait()

        def some(q, c):
            for i in range(4):
                g = q * 4 + i
                at = pl.ds(pl.multiple_of(g * 16, 16), 16)
                right = jnp.concatenate([tiles[g * group + j] for j in range(group)], axis=1)
                value = chosen(dot(lhs[at], right))
                part_out[t, at] = value
            return c

        lax.fori_loop(0, groups // 4, some, 0)

        @pl.when(bin_at == 1)
        def _():
            for k in range(3, bins, 2):
                part(t, k).wait_recv()
                part_out[t] += part_in[t, k]

        @pl.when(bin_at > 0)
        def _():
            part(t, bin_at).start()

        @pl.when(bin_at == 0)
        def _():
            value = part_out[t]
            for k in [*range(2, bins, 2), 1]:
                part(t, k).wait_recv()
                value = value + part_in[t, k]
            driven[t] = (excitation[t] - value).astype(BF16)
            for d in range(1, bins):
                tell(t, d).start()

            @pl.when(t == 0)
            def _():
                loads[2].wait()

            solve(t)

        return carry

    lax.fori_loop(0, steps, step, 0)

    @pl.when(bin_at > 0)
    def _():
        def last(u, c):
            @pl.when(u >= steps - 1 - bin_at)
            def _():
                tell(u, 0).wait_recv()

                @pl.when(u == 0)
                def _():
                    loads[2].wait()

                solve(u)
            return c

        lax.fori_loop(0, steps, last, 0)

    for d in range(1, readers):
        ask(d).wait_send()
    for s in range(1, min(steps, bins)):
        @pl.when(bin_at + s < bins)
        def _():
            shift(s).wait_send()

    def drain(t, c):
        for d in range(1, readers):
            swap(t, d).wait_send()

        @pl.when(bin_at > 0)
        def _():
            part(t, bin_at).wait_send()

        @pl.when(bin_at == 0)
        def _():
            for d in range(1, bins):
                tell(t, d).wait_send()
        return c

    lax.fori_loop(0, steps, drain, 0)


def body(retarded_tiles, wanted_blocks, tile_slots, diag_inverse, excitation, history_init):
    readers, bins = lax.axis_size("rows"), lax.axis_size("delay")
    _, n, listed, width, _ = retarded_tiles.shape
    steps, _, exc, _ = excitation.shape
    cap = wanted_blocks.shape[-1]
    rows, taken = n * exc, readers * cap * exc
    sizes = (readers, bins, steps, n, listed, exc, cap, width)
    vmem = pl.BlockSpec(memory_space=pltpu.VMEM)
    anywhere = pl.BlockSpec(memory_space=pltpu.HBM)
    dma = pltpu.SemaphoreType.DMA
    solved = pl.pallas_call(
        functools.partial(kernel, sizes),
        out_shape=pltpu.VMEM((steps, rows, width), F32),
        in_specs=[anywhere] * 6,
        out_specs=vmem,
        scratch_shapes=[
            pltpu.VMEM((readers, cap), jnp.int32),
            pltpu.VMEM((listed, n), jnp.int32),
            pltpu.VMEM((n, listed * width, width), BF16),
            pltpu.VMEM((n, width, width), BF16),
            pltpu.VMEM((steps, rows, width), F32),
            pltpu.VMEM((taken, rows), BF16),
            pltpu.VMEM((listed, rows, taken), BF16),
            pltpu.VMEM((readers * cap, width), F32),
            pltpu.VMEM((readers * cap, width), F32),
            pltpu.VMEM((steps + 1, rows, width), BF16),
            pltpu.VMEM((steps, taken, width), BF16),
            pltpu.VMEM((steps, taken, width), BF16),
            pltpu.VMEM((rows, listed * width), BF16),
            pltpu.VMEM((steps, rows, width), F32),
            pltpu.VMEM((steps, bins, rows, width), F32),
            pltpu.VMEM((steps, rows, width), BF16),
            dma((6,)),
            dma((readers,)),
            dma((readers,)),
            dma((steps,)),
            dma((steps,)),
            dma((steps, readers)),
            dma((steps, readers)),
            dma((steps,)),
            dma((steps, bins)),
            dma((steps, bins)),
            dma((steps,)),
        ],
        compiler_params=pltpu.CompilerParams(
            collective_id=0, has_side_effects=True, vmem_limit_bytes=57 << 20
        ),
        cost_estimate=pl.CostEstimate(
            flops=2 * steps * rows * width * width * (listed + 1), transcendentals=0,
            bytes_accessed=2 * n * width * width * (listed + 1),
        ),
    )(
        history_init.reshape(rows, width),
        wanted_blocks.reshape(readers, cap),
        tile_slots.reshape(n, listed).T,
        retarded_tiles.reshape(n, listed * width, width),
        diag_inverse,
        excitation.reshape(steps, rows, width),
    )
    return solved.reshape(steps, n, exc, width)


def solution(mesh):
    return jax.shard_map(
        body,
        mesh=mesh,
        in_specs=(
            P("delay", "rows", None, None, None),
            P("delay", "rows", None, None),
            P("delay", "rows", None),
            P("rows", None, None),
            P(None, "rows", None, None),
            P("delay", "rows", None, None),
        ),
        out_specs=P(None, "rows", None, None),
        check_vma=False,
    )
```
